32 devices in a mesh: fsdp: 4 (over z), ctx: 4 (over x, core), tp: 2 (over y).
Axes of the slice: x: 2, y: 2, z: 4, core: 2. Of those that a mesh axis runs over, the one named last changes fastest.
Arguments:
- tokens: bfloat16 [12, 1152, 1024], P('fsdp', 'ctx'), may hold values from -6 to 6
- segment_ids: int32 [12, 1152], P('fsdp'), may hold values from 0 to 3, as said below
- first_gain: float32 [1024], replicated, may hold values from 0.5 to 1.5
- first_shift: float32 [1024], replicated, may hold values from -1 to 1
- qkv_weight: bfloat16 [3, 1024, 1024], P(None, ('fsdp', 'ctx'), 'tp'), may hold values from -0.1875 to 0.1875
- qv_bias: float32 [2, 1024], P(None, 'tp'), may hold values from -1 to 1
- out_weight: bfloat16 [1024, 1024], P('tp', ('fsdp', 'ctx')), may hold values from -1.5 to 1.5
- out_bias: float32 [1024], replicated, may hold values from -1 to 1
- second_gain: float32 [1024], replicated, may hold values from 0.5 to 1.5
- second_shift: float32 [1024], replicated, may hold values from -1 to 1
- up_weight: bfloat16 [1024, 4096], P(('fsdp', 'ctx'), 'tp'), may hold values from -0.1875 to 0.1875
- up_bias: float32 [4096], P('tp'), may hold values from -1 to 1
- down_weight: bfloat16 [4096, 1024], P('tp', ('fsdp', 'ctx')), may hold values from -0.09375 to 0.09375
- down_bias: float32 [1024], replicated, may hold values from -1 to 1
- cotangent: bfloat16 [12, 1152, 1024], P('fsdp', 'ctx'), may hold values from -6 to 6
Outputs:
- layer_out: bfloat16 [12, 1152, 1024], P('fsdp', 'ctx')
- grad_tokens: float32 [12, 1152, 1024], P('fsdp', 'ctx')
- grad_first_gain: float32 [1024], replicated
- grad_first_shift: float32 [1024], replicated
- grad_qkv_weight: float32 [3, 1024, 1024], P(None, ('fsdp', 'ctx'), 'tp')
- grad_qv_bias: float32 [2, 1024], P(None, 'tp')
- grad_out_weight: float32 [1024, 1024], P('tp', ('fsdp', 'ctx'))
- grad_out_bias: float32 [1024], replicated
- grad_second_gain: float32 [1024], replicated
- grad_second_shift: float32 [1024], replicated
- grad_up_weight: float32 [1024, 4096], P(('fsdp', 'ctx'), 'tp')
- grad_up_bias: float32 [4096], P('tp')
- grad_down_weight: float32 [4096, 1024], P('tp', ('fsdp', 'ctx'))
- grad_down_bias: float32 [1024], replicated
The draws below stay inside these ranges and needn't reach their ends.
Inputs may be any that keep to these rules, and one draw needn't show every extreme that they name: `segment_ids`: along each sequence the segment numbers never fall and start at 0. In each aligned block of 3 sequences one sequence is a single segment; in every other sequence the numbers rise by 3 in all.
All inputs are finite; a program needn't handle non-finite values.
Results may differ from the reference program's by a relative error of at most 0.013.
Values may be sent and summed in bfloat16 or wider, within the bound.
A program may use at most 192 MiB of HBM per device.

```python
import jax
import jax.numpy as jnp
from jax import lax

D = 1024
H = 16
HD = 64
FF = 4096
SEQS = 3
QBLK = 576
NSEQ = 12
LENGTH = 1152


def draw_segment_ids(key, part):
    key = jax.random.fold_in(key, 7)
    cut_key, pick_key = jax.random.split(key)
    cut_points = jax.random.randint(cut_key, (NSEQ, 3), 1, LENGTH)
    picked = jax.random.randint(pick_key, (NSEQ // SEQS,), 0, SEQS)
    seq_index = jnp.arange(NSEQ, dtype=jnp.int32)
    single = seq_index % SEQS == picked[seq_index // SEQS]
    cut_points = jnp.where(single[:, None], LENGTH, cut_points)
    positions = jnp.arange(LENGTH, dtype=jnp.int32)
    return jnp.sum((positions[None, :, None] >= cut_points[:, None, :]).astype(jnp.int32), -1)


def block_levels(key, dims, pieces, low, largest):
    level = 1.0
    for position, parts in pieces:
        draws = jax.random.uniform(jax.random.fold_in(jax.random.fold_in(key, 6), position), (parts,), jnp.float32, low / len(pieces), largest / len(pieces))
        level = level * jnp.repeat(jnp.exp(draws), dims[position] // parts).reshape((-1,) + (1,) * (len(dims) - 1 - position))
    return level


def noise(stream_key, extent, scale, bound, cuts=(), kind=jnp.bfloat16):
    values = jax.random.normal(stream_key, extent, jnp.float32) * scale
    if len(cuts) > 0:
        values = block_levels(stream_key, extent, cuts, -0.22, 0.18) * values
    return jnp.clip(values, min=-bound, max=bound).astype(kind)


def setup_inputs(seed: int = 0) -> dict:
    splits = jax.random.split(jax.random.key(seed), 16)
    return {
        "tokens": noise(splits[0], (NSEQ, LENGTH, D), 1.0, 6.0, ((0, 4), (1, 4))),
        "segment_ids": draw_segment_ids(jax.random.fold_in(splits[15], 71), 0),
        "first_gain": jnp.clip(1.0 + 0.1 * jax.random.normal(splits[2], (D,), jnp.float32), 0.5, 1.5),
        "first_shift": noise(splits[3], (D,), 0.2, 1.0, (), jnp.float32),
        "qkv_weight": noise(splits[4], (3, D, D), D ** -0.5, 0.1875, ((1, 16), (2, 2))),
        "qv_bias": noise(splits[5], (2, D), 0.2, 1.0, ((1, 2),), jnp.float32),
        "out_weight": noise(splits[6], (D, D), 16 ** -0.5, 1.5, ((0, 2), (1, 16))),
        "out_bias": noise(splits[7], (D,), 0.2, 1.0, (), jnp.float32),
        "second_gain": jnp.clip(1.0 + 0.1 * jax.random.normal(splits[8], (D,), jnp.float32), 0.5, 1.5),
        "second_shift": noise(splits[9], (D,), 0.2, 1.0, (), jnp.float32),
        "up_weight": noise(splits[10], (D, FF), D ** -0.5, 0.1875, ((0, 16), (1, 2))),
        "up_bias": noise(splits[11], (FF,), 0.2, 1.0, ((0, 2),), jnp.float32),
        "down_weight": noise(splits[12], (FF, D), FF ** -0.5, 0.09375, ((0, 2), (1, 16))),
        "down_bias": noise(splits[13], (D,), 0.2, 1.0, (), jnp.float32),
        "cotangent": noise(splits[14], (NSEQ, LENGTH, D), 1.0, 6.0, ((0, 4), (1, 4))),
    }


EPS = 1e-05
MASKED = -1e+30
HIGH = lax.Precision.HIGHEST

@jax.custom_vjp
def low(v):
    return lax.optimization_barrier(v.astype(jnp.bfloat16)).astype(jnp.float32)

@jax.custom_vjp
def low_back(v):
    return v

def low_keep(v):
    return (low(v), None)

def low_pass(kept, grad):
    return (grad,)

def back_keep(v):
    return (v, None)

def back_low(kept, grad):
    return (low(grad),)
low.defvjp(low_keep, low_pass)
low_back.defvjp(back_keep, back_low)

def layer_norm(values, gain, shift):
    centred = values - lax.optimization_barrier(jnp.mean(values, -1, keepdims=True))
    spread = lax.optimization_barrier(jnp.mean(centred * centred, -1, keepdims=True))
    return centred * lax.rsqrt(spread + EPS) * gain + shift

def attend(queries, key_heads, value_heads, segments):
    seq_len = queries.shape[0]
    positions = jnp.arange(seq_len, dtype=jnp.int32)

    def one_block(block_index):
        block_start = block_index * QBLK
        block_queries = lax.dynamic_slice_in_dim(queries, block_start, QBLK, 0)
        block_segments = lax.dynamic_slice_in_dim(segments, block_start, QBLK, 0)
        row_pos = block_start + jnp.arange(QBLK, dtype=jnp.int32)
        allowed = (row_pos[:, None] >= positions[None, :]) & (block_segments[:, None] == segments[None, :])
        scores = jnp.einsum('qhd,khd->hqk', block_queries, key_heads, precision=HIGH) * HD ** (-0.5)
        scores = low_back(scores)
        scores = jnp.where(allowed[None], scores, MASKED)
        highest = lax.optimization_barrier(jnp.max(scores, -1, keepdims=True))
        raised = jnp.exp(scores - highest)
        softmaxed = raised / lax.optimization_barrier(jnp.sum(raised, -1, keepdims=True))
        return jnp.einsum('hqk,khd->qhd', low(softmaxed), value_heads, precision=HIGH)
    blocks = lax.map(jax.checkpoint(one_block), jnp.arange(seq_len // QBLK, dtype=jnp.int32))
    return blocks.reshape(seq_len, H * HD)

def forward(values, segments, params):
    gain_one, shift_one, qkv_w, qv_b, out_w, out_b, gain_two, shift_two, up_w, up_b, down_w, down_b = params
    seq_len = values.shape[0]
    first_in = low(layer_norm(values, gain_one, shift_one))
    projected = jnp.einsum('td,jde->tje', first_in, qkv_w, precision=HIGH)
    bias_rows = jnp.stack([qv_b[0], jnp.zeros_like(qv_b[0]), qv_b[1]])
    projected = low_back(low(projected + bias_rows))
    split_heads = projected.reshape(seq_len, 3, H, HD)
    attended = attend(split_heads[:, 0], split_heads[:, 1], split_heads[:, 2], segments)
    attended = low_back(low(attended))
    middle = values + low_back(jnp.dot(attended, out_w, precision=HIGH)) + out_b
    second_in = low(layer_norm(middle, gain_two, shift_two))
    hidden_pre = low_back(jnp.dot(second_in, up_w, precision=HIGH)) + up_b
    hidden = low(jax.nn.gelu(hidden_pre, approximate=True))
    return middle + low_back(jnp.dot(hidden, down_w, precision=HIGH)) + down_b

def reference(tokens, segment_ids, first_gain, first_shift, qkv_weight, qv_bias, out_weight, out_bias, second_gain, second_shift, up_weight, up_bias, down_weight, down_bias, cotangent):
    params = tuple((member.astype(jnp.float32) for member in (first_gain, first_shift, qkv_weight, qv_bias, out_weight, out_bias, second_gain, second_shift, up_weight, up_bias, down_weight, down_bias)))

    def step(carried, member):
        seq_tokens, seq_segments, seq_cot = member
        result, pull = jax.vjp(lambda values, weights: forward(values, seq_segments, weights), seq_tokens.astype(jnp.float32), params)
        grad_values, grad_params = pull(seq_cot.astype(jnp.float32))
        carried = jax.tree.map(jnp.add, carried, grad_params)
        return (carried, (result.astype(jnp.bfloat16), grad_values))
    empty = jax.tree.map(jnp.zeros_like, params)
    totals, (layer_out, grad_tokens) = lax.scan(step, empty, (tokens, segment_ids, cotangent))
    g_one, s_one, g_qkv, g_qv, g_out, g_outb, g_two, s_two, g_up, g_upb, g_down, g_downb = totals
    return (layer_out, grad_tokens, g_one, s_one, g_qkv, g_qv, g_out, g_outb, g_two, s_two, g_up, g_upb, g_down, g_downb)
```

```python
import functools

import jax
import jax.numpy as jnp
import numpy as np
from jax import lax
from jax.experimental import pallas as pl
from jax.experimental.pallas import tpu as pltpu
from jax.sharding import Mesh
from jax.sharding import PartitionSpec as P

HD = 64
EPS = 1e-05
MASKED = -1e30
LOG2E = 1.4426950408889634
BF = jnp.bfloat16
F32 = jnp.float32
CTX = ("x", "core")
SAME = ("fsdp", "x")
ALL = ("fsdp", "x", "core")


def smooth_gate(values):
    return jax.nn.gelu(values, approximate=True)


def norm_forward(values, gain, shift):
    centred = values - jnp.mean(values, -1, keepdims=True)
    spread = jnp.mean(centred * centred, -1, keepdims=True)
    inverse = lax.rsqrt(spread + EPS)
    normed = centred * inverse
    return (normed * gain + shift, normed, inverse)


def norm_backward(grad, normed, inverse, gain):
    grad_gain = jnp.sum(grad * normed, axis=(0, 1))
    grad_shift = jnp.sum(grad, axis=(0, 1))
    scaled = grad * gain
    first_mean = jnp.mean(scaled, -1, keepdims=True)
    second_mean = jnp.mean(scaled * normed, -1, keepdims=True)
    return (inverse * (scaled - first_mean - normed * second_mean), grad_gain, grad_shift)


def dot(a, b, da, db):
    return lax.dot_general(a, b, (((da,), (db,)), ((), ())), preferred_element_type=F32)


def query_block(seq_len):
    for size in (384, 256, 128, 64, 32, 16):
        if seq_len % size == 0:
            return size
    return seq_len


def masked_scores(k, q, start, first):
    keys, rows = k.shape[0], q.shape[0]
    scores = dot(k, q, 1, 1) * (HD ** (-0.5) * LOG2E)
    key_pos = lax.broadcasted_iota(jnp.int32, (keys, rows), 0)
    row_pos = first + lax.broadcasted_iota(jnp.int32, (1, rows), 1)
    allowed = (key_pos >= start) & (key_pos <= row_pos)
    return jnp.where(allowed, scores, MASKED)


def forward_kernel(q_ref, k_ref, v_ref, start_ref, out_ref, lse_ref):
    seq_len, width = q_ref.shape[1:]
    block = query_block(seq_len)
    for first in range(0, seq_len, block):
        rows = slice(first, first + block)
        keys = slice(0, first + block)
        start = start_ref[0, :, rows]
        for head in range(width // HD):
            cols = slice(head * HD, (head + 1) * HD)
            scores = masked_scores(k_ref[0, keys, cols], q_ref[0, rows, cols], start, first)
            highest = jnp.max(scores, 0, keepdims=True)
            raised = jnp.exp2(scores - highest)
            summed = jnp.sum(raised, 0, keepdims=True)
            probs = (raised * (1.0 / summed)).astype(BF)
            out_ref[0, rows, cols] = dot(probs, v_ref[0, keys, cols], 0, 0).astype(BF)
            lse_ref[0, head : head + 1, rows] = highest + jnp.log2(summed)


def backward_kernel(q_ref, k_ref, v_ref, start_ref, lse_ref, g_ref, dq_ref, dk_ref, dv_ref, ak, av):
    seq_len, width = q_ref.shape[1:]
    block = query_block(seq_len)
    ak[...] = jnp.zeros_like(ak)
    av[...] = jnp.zeros_like(av)
    for first in range(0, seq_len, block):
        rows = slice(first, first + block)
        keys = slice(0, first + block)
        start = start_ref[0, :, rows]
        for head in range(width // HD):
            cols = slice(head * HD, (head + 1) * HD)
            k, q, g = k_ref[0, keys, cols], q_ref[0, rows, cols], g_ref[0, rows, cols]
            scores = masked_scores(k, q, start, first)
            probs = jnp.exp2(scores - lse_ref[0, head : head + 1, rows])
            grad_probs = dot(v_ref[0, keys, cols], g, 1, 1)
            row_dot = jnp.sum(probs * grad_probs, 0, keepdims=True)
            grad_scores = (probs * (grad_probs - row_dot)).astype(BF)
            dq_ref[0, rows, cols] = (dot(grad_scores, k, 0, 0) * HD ** (-0.5)).astype(BF)
            ak[head, keys, :] += dot(grad_scores, q, 1, 0)
            av[head, keys, :] += dot(probs.astype(BF), g, 1, 0)
    for head in range(width // HD):
        cols = slice(head * HD, (head + 1) * HD)
        dk_ref[0, :, cols] = (ak[head] * HD ** (-0.5)).astype(BF)
        dv_ref[0, :, cols] = av[head].astype(BF)


def part_spec(seq_len, width, part):
    return pl.BlockSpec((1, seq_len, width), lambda s: (s, 0, part))


def attend_forward(q, k, v, start):
    seqs, seq_len, width = q.shape
    heads = width // HD
    whole = pl.BlockSpec((1, seq_len, width), lambda s: (s, 0, 0))
    row = pl.BlockSpec((1, 1, seq_len), lambda s: (s, 0, 0))
    lse = pl.BlockSpec((1, heads, seq_len), lambda s: (s, 0, 0))
    square = seqs * heads * seq_len * seq_len
    return pl.pallas_call(
        forward_kernel,
        grid=(seqs,),
        in_specs=[whole, whole, whole, row],
        out_specs=[whole, lse],
        out_shape=[
            jax.ShapeDtypeStruct((seqs, seq_len, width), BF),
            jax.ShapeDtypeStruct((seqs, heads, seq_len), F32),
        ],
        compiler_params=pltpu.CompilerParams(vmem_limit_bytes=40 * 1024 * 1024),
        cost_estimate=pl.CostEstimate(
            flops=square * HD * 16, bytes_accessed=seqs * seq_len * width * 8, transcendentals=square
        ),
    )(q, k, v, start)


def attend_backward(q, k, v, start, lses, grads):
    seqs, seq_len, width = q.shape
    heads = width // HD
    whole = pl.BlockSpec((1, seq_len, width), lambda s: (s, 0, 0))
    row = pl.BlockSpec((1, 1, seq_len), lambda s: (s, 0, 0))
    lse = pl.BlockSpec((1, heads, seq_len), lambda s: (s, 0, 0))
    square = seqs * heads * seq_len * seq_len
    shape = jax.ShapeDtypeStruct((seqs, seq_len, width), BF)
    return pl.pallas_call(
        backward_kernel,
        grid=(seqs,),
        in_specs=[whole, whole, whole, row, lse, whole],
        out_specs=[whole, whole, whole],
        out_shape=[shape, shape, shape],
        scratch_shapes=[
            pltpu.VMEM((heads, seq_len, HD), F32),
            pltpu.VMEM((heads, seq_len, HD), F32),
        ],
        compiler_params=pltpu.CompilerParams(vmem_limit_bytes=40 * 1024 * 1024),
        cost_estimate=pl.CostEstimate(
            flops=square * HD * 40, bytes_accessed=seqs * seq_len * width * 14, transcendentals=square
        ),
    )(q, k, v, start, lses, grads)


def swap(values, axis):
    count = lax.axis_size(axis)
    return lax.ppermute(values, axis, [(i, i ^ 1) for i in range(count)])


def pair_sum(values):
    sent = values.astype(BF)
    return sent.astype(F32) + swap(sent, "tp").astype(F32)


def gather_rows(shard):
    part = lax.all_gather(shard, SAME, axis=0, tiled=False)
    other = swap(part, "core")
    core = lax.axis_index("core")
    low = jnp.where(core == 0, part, other)
    high = jnp.where(core == 0, other, part)
    return jnp.stack([low, high], axis=1).reshape(-1, shard.shape[1])


def scatter_rows(grad):
    groups = lax.axis_size("fsdp") * lax.axis_size("x")
    rows = grad.shape[0] // (2 * groups)
    core = lax.axis_index("core")
    halves = grad.astype(BF).reshape(groups, 2, rows, grad.shape[1])
    mine = lax.dynamic_index_in_dim(halves, core, 1, keepdims=False)
    theirs = lax.dynamic_index_in_dim(halves, 1 - core, 1, keepdims=False)
    summed = (mine.astype(F32) + swap(theirs, "core").astype(F32)).astype(BF)
    summed = summed.reshape(groups * rows, grad.shape[1])
    return lax.psum_scatter(summed, SAME, scatter_dimension=0, tiled=True).astype(F32)


def small_sums(*vectors):
    flat = jnp.concatenate([v.reshape(-1) for v in vectors])
    total = jnp.sum(lax.all_gather(flat, ALL, axis=0, tiled=False), 0)
    outs, at = [], 0
    for v in vectors:
        outs.append(total[at : at + v.size].reshape(v.shape))
        at += v.size
    return outs


def local(
    tokens,
    segment_ids,
    first_gain,
    first_shift,
    qkv_weight,
    qv_bias,
    out_weight,
    out_bias,
    second_gain,
    second_shift,
    up_weight,
    up_bias,
    down_weight,
    down_bias,
    cotangent,
):
    seqs, local_len, model = tokens.shape
    seq_len = segment_ids.shape[1]
    heads_cols = qkv_weight.shape[2]
    rows = seqs * local_len
    barrier = lax.optimization_barrier
    qkv_rows = jnp.moveaxis(qkv_weight, 0, 1).reshape(qkv_weight.shape[1], 3 * heads_cols)
    w_qkv = gather_rows(qkv_rows)
    w_out = gather_rows(out_weight.T)
    w_up = gather_rows(up_weight)
    w_down = gather_rows(down_weight.T)

    start = jnp.sum(
        (segment_ids[:, None, :] < segment_ids[:, :, None]).astype(jnp.int32), -1
    )[:, None, :]
    inputs = tokens.astype(F32)
    normed_in, normed_one, inverse_one = norm_forward(inputs, first_gain, first_shift)
    first_in = normed_in.astype(BF)
    bias_row = jnp.concatenate([qv_bias[0], jnp.zeros_like(qv_bias[0]), qv_bias[1]])
    projected = (dot(first_in.reshape(rows, model), w_qkv, 1, 0) + bias_row).astype(BF)
    projected = projected.reshape(seqs, local_len, 3, heads_cols)
    by_heads = lax.all_to_all(projected, CTX, split_axis=3, concat_axis=1, tiled=True)
    q, k, v = by_heads[:, :, 0], by_heads[:, :, 1], by_heads[:, :, 2]
    attended, lses = attend_forward(q, k, v, start)
    mixed = lax.all_to_all(attended, CTX, split_axis=1, concat_axis=2, tiled=True)
    mixed_rows = mixed.reshape(rows, heads_cols)

    attn_part = dot(mixed_rows, w_out, 1, 1).reshape(seqs, local_len, model)
    cot_rows = cotangent.reshape(rows, model)
    middle = inputs + pair_sum(attn_part) + out_bias
    normed_mid, normed_two, inverse_two = norm_forward(middle, second_gain, second_shift)
    second_in = normed_mid.astype(BF).reshape(rows, model)
    hidden_pre = dot(second_in, w_up, 1, 0) + up_bias
    activated, gate_pull = jax.vjp(smooth_gate, hidden_pre)
    hidden = activated.astype(BF)
    grad_hidden = dot(cot_rows, w_down, 1, 0)
    grad_pre = gate_pull(grad_hidden)[0]
    grad_pre_low = grad_pre.astype(BF)
    grad_up_b = jnp.sum(grad_pre, axis=0)
    grad_two_sum = pair_sum(dot(grad_pre_low, w_up, 1, 1).reshape(seqs, local_len, model))
    grad_top = cotangent.astype(F32)
    grad_mid_norm, grad_gain_two, grad_shift_two = norm_backward(
        grad_two_sum, normed_two, inverse_two, second_gain
    )
    grad_mid = grad_top + grad_mid_norm
    grad_mid_low = grad_mid.astype(BF).reshape(rows, model)
    grad_mixed = dot(grad_mid_low, w_out, 1, 0).astype(BF).reshape(seqs, local_len, heads_cols)

    grad_down = dot(cot_rows, hidden, 0, 0).astype(BF)
    grad_up = dot(second_in, grad_pre_low, 0, 0).astype(BF)
    grad_out = dot(grad_mid_low, mixed_rows, 0, 0).astype(BF)
    down_part = dot(hidden, w_down, 1, 1).reshape(seqs, local_len, model)

    grad_att = lax.all_to_all(grad_mixed, CTX, split_axis=2, concat_axis=1, tiled=True)
    grad_att, grad_down, grad_up, grad_out, down_part = barrier(
        (grad_att, grad_down, grad_up, grad_out, down_part.astype(BF))
    )
    layer_out = (middle + pair_sum(down_part) + down_bias).astype(BF)
    dq, dk, dv = attend_backward(q, k, v, start, lses, grad_att)
    grad_heads = jnp.stack([dq, dk, dv], axis=2)
    grad_proj = lax.all_to_all(grad_heads, CTX, split_axis=1, concat_axis=3, tiled=True)
    grad_proj = grad_proj.reshape(rows, 3 * heads_cols)
    grad_one_part = dot(grad_proj, w_qkv, 1, 1).reshape(seqs, local_len, model)
    grad_one_sum = pair_sum(grad_one_part)
    grad_qkv = dot(first_in.reshape(rows, model), grad_proj, 0, 0)
    grad_in_norm, grad_gain_one, grad_shift_one = norm_backward(
        grad_one_sum, normed_one, inverse_one, first_gain
    )
    grad_inputs = grad_mid + grad_in_norm

    own_down = scatter_rows(grad_down).T
    own_up = scatter_rows(grad_up)
    own_out = scatter_rows(grad_out).T
    own_qkv = scatter_rows(grad_qkv)
    own_qkv = jnp.moveaxis(own_qkv.reshape(-1, 3, heads_cols), 1, 0)
    grad_qv_b = jnp.sum(grad_proj.astype(F32), axis=0).reshape(3, heads_cols)[0::2]
    sum_up_b, sum_down_b, sum_out_b, sum_gain_two, sum_shift_two = small_sums(
        grad_up_b,
        jnp.sum(grad_top, axis=(0, 1)),
        jnp.sum(grad_mid, axis=(0, 1)),
        grad_gain_two,
        grad_shift_two,
    )
    sum_qv_b, sum_gain_one, sum_shift_one = small_sums(grad_qv_b, grad_gain_one, grad_shift_one)
    return (
        layer_out,
        grad_inputs,
        sum_gain_one,
        sum_shift_one,
        own_qkv,
        sum_qv_b,
        own_out,
        sum_out_b,
        sum_gain_two,
        sum_shift_two,
        own_up,
        sum_up_b,
        own_down,
        sum_down_b,
    )


def solution(mesh):
    sizes = mesh.shape
    fine = Mesh(
        np.asarray(mesh.devices).reshape(sizes["fsdp"], sizes["ctx"] // 2, 2, sizes["tp"]),
        ("fsdp", "x", "core", "tp"),
    )
    return jax.shard_map(
        local,
        mesh=fine,
        in_specs=(
            P("fsdp", CTX, None),
            P("fsdp", None),
            P(),
            P(),
            P(None, ALL, "tp"),
            P(None, "tp"),
            P("tp", ALL),
            P(),
            P(),
            P(),
            P(ALL, "tp"),
            P("tp"),
            P("tp", ALL),
            P(),
            P("fsdp", CTX, None),
        ),
        out_specs=(
            P("fsdp", CTX, None),
            P("fsdp", CTX, None),
            P(),
            P(),
            P(None, ALL, "tp"),
            P(None, "tp"),
            P("tp", ALL),
            P(),
            P(),
            P(),
            P(ALL, "tp"),
            P("tp"),
            P("tp", ALL),
            P(),
        ),
        check_vma=False,
    )
```

```python
import functools

import jax
import jax.numpy as jnp
import numpy as np
from jax import lax
from jax.experimental import pallas as pl
from jax.experimental.pallas import tpu as pltpu
from jax.sharding import Mesh
from jax.sharding import PartitionSpec as P

HD = 64
EPS = 1e-05
MASKED = -1e30
LOG2E = 1.4426950408889634
BF = jnp.bfloat16
F32 = jnp.float32
CTX = ("x", "core")
SAME = ("fsdp", "x")
ALL = ("fsdp", "x", "core")


def smooth_gate(values):
    return jax.nn.gelu(values, approximate=True)


def norm_forward(values, gain, shift):
    centred = values - jnp.mean(values, -1, keepdims=True)
    spread = jnp.mean(centred * centred, -1, keepdims=True)
    inverse = lax.rsqrt(spread + EPS)
    normed = centred * inverse
    return (normed * gain + shift, normed, inverse)


def norm_backward(grad, normed, inverse, gain):
    grad_gain = jnp.sum(grad * normed, axis=(0, 1))
    grad_shift = jnp.sum(grad, axis=(0, 1))
    scaled = grad * gain
    first_mean = jnp.mean(scaled, -1, keepdims=True)
    second_mean = jnp.mean(scaled * normed, -1, keepdims=True)
    return (inverse * (scaled - first_mean - normed * second_mean), grad_gain, grad_shift)


def dot(a, b, da, db):
    return lax.dot_general(a, b, (((da,), (db,)), ((), ())), preferred_element_type=F32)


def query_block(seq_len):
    for size in (384, 256, 128, 64, 32, 16):
        if seq_len % size == 0:
            return size
    return seq_len


def masked_scores(k, q, start, first):
    keys, rows = k.shape[0], q.shape[0]
    scores = dot(k, q, 1, 1) * (HD ** (-0.5) * LOG2E)
    key_pos = lax.broadcasted_iota(jnp.int32, (keys, rows), 0)
    row_pos = first + lax.broadcasted_iota(jnp.int32, (1, rows), 1)
    allowed = (key_pos >= start) & (key_pos <= row_pos)
    return jnp.where(allowed, scores, MASKED)


def forward_kernel(qkv_ref, start_ref, out_ref, lse_ref, out):
    parts, _, local_len, triple = qkv_ref.shape
    seq_len, width = parts * local_len, triple // 3
    block = query_block(seq_len)
    qkv = qkv_ref[...].reshape(seq_len, triple)
    for first in range(0, seq_len, block):
        rows = slice(first, first + block)
        keys = slice(0, first + block)
        start = start_ref[0, :, rows]
        for head in range(width // HD):
            at = head * HD
            q, k, v = (
                qkv[span, j * width + at : j * width + at + HD]
                for j, span in enumerate((rows, keys, keys))
            )
            scores = masked_scores(k, q, start, first)
            highest = jnp.max(scores, 0, keepdims=True)
            raised = jnp.exp2(scores - highest)
            summed = jnp.sum(raised, 0, keepdims=True)
            probs = (raised * (1.0 / summed)).astype(BF)
            out[rows, at : at + HD] = dot(probs, v, 0, 0).astype(BF)
            lse_ref[0, head : head + 1, rows] = highest + jnp.log2(summed)
    out_ref[...] = out[...].reshape(out_ref.shape)


def backward_kernel(qkv_ref, start_ref, lse_ref, g_ref, out_ref, out, ak, av):
    parts, _, local_len, triple = qkv_ref.shape
    seq_len, width = parts * local_len, triple // 3
    block = query_block(seq_len)
    qkv = qkv_ref[...].reshape(seq_len, triple)
    grads = g_ref[...].reshape(seq_len, width)
    ak[...] = jnp.zeros_like(ak)
    av[...] = jnp.zeros_like(av)
    for first in range(0, seq_len, block):
        rows = slice(first, first + block)
        keys = slice(0, first + block)
        start = start_ref[0, :, rows]
        for head in range(width // HD):
            at = head * HD
            q, k, v = (
                qkv[span, j * width + at : j * width + at + HD]
                for j, span in enumerate((rows, keys, keys))
            )
            g = grads[rows, at : at + HD]
            scores = masked_scores(k, q, start, first)
            probs = jnp.exp2(scores - lse_ref[0, head : head + 1, rows])
            grad_probs = dot(v, g, 1, 1)
            row_dot = jnp.sum(probs * grad_probs, 0, keepdims=True)
            grad_scores = (probs * (grad_probs - row_dot)).astype(BF)
            out[rows, at : at + HD] = (dot(grad_scores, k, 0, 0) * HD ** (-0.5)).astype(BF)
            ak[head, keys, :] += dot(grad_scores, q, 1, 0)
            av[head, keys, :] += dot(probs.astype(BF), g, 1, 0)
    for head in range(width // HD):
        at = width + head * HD
        out[:, at : at + HD] = (ak[head] * HD ** (-0.5)).astype(BF)
        out[:, at + width : at + width + HD] = av[head].astype(BF)
    out_ref[...] = out[...].reshape(out_ref.shape)


def attend_forward(qkv, start):
    parts, seqs, local_len, triple = qkv.shape
    seq_len, width = parts * local_len, triple // 3
    heads = width // HD
    square = seqs * heads * seq_len * seq_len
    return pl.pallas_call(
        forward_kernel,
        grid=(seqs,),
        in_specs=[
            pl.BlockSpec((parts, 1, local_len, triple), lambda s: (0, s, 0, 0)),
            pl.BlockSpec((1, 1, seq_len), lambda s: (s, 0, 0)),
        ],
        out_specs=[
            pl.BlockSpec((parts, 1, local_len, width), lambda s: (0, s, 0, 0)),
            pl.BlockSpec((1, heads, seq_len), lambda s: (s, 0, 0)),
        ],
        out_shape=[
            jax.ShapeDtypeStruct((parts, seqs, local_len, width), BF),
            jax.ShapeDtypeStruct((seqs, heads, seq_len), F32),
        ],
        scratch_shapes=[pltpu.VMEM((seq_len, width), BF)],
        compiler_params=pltpu.CompilerParams(vmem_limit_bytes=40 * 1024 * 1024),
        cost_estimate=pl.CostEstimate(
            flops=square * HD * 16, bytes_accessed=seqs * seq_len * width * 8, transcendentals=square
        ),
    )(qkv, start)


def attend_backward(qkv, start, lses, grads):
    parts, seqs, local_len, triple = qkv.shape
    seq_len, width = parts * local_len, triple // 3
    heads = width // HD
    square = seqs * heads * seq_len * seq_len
    wide = pl.BlockSpec((parts, 1, local_len, triple), lambda s: (0, s, 0, 0))
    return pl.pallas_call(
        backward_kernel,
        grid=(seqs,),
        in_specs=[
            wide,
            pl.BlockSpec((1, 1, seq_len), lambda s: (s, 0, 0)),
            pl.BlockSpec((1, heads, seq_len), lambda s: (s, 0, 0)),
            pl.BlockSpec((parts, 1, local_len, width), lambda s: (0, s, 0, 0)),
        ],
        out_specs=wide,
        out_shape=jax.ShapeDtypeStruct(qkv.shape, BF),
        scratch_shapes=[
            pltpu.VMEM((seq_len, triple), BF),
            pltpu.VMEM((heads, seq_len, HD), F32),
            pltpu.VMEM((heads, seq_len, HD), F32),
        ],
        compiler_params=pltpu.CompilerParams(vmem_limit_bytes=40 * 1024 * 1024),
        cost_estimate=pl.CostEstimate(
            flops=square * HD * 40, bytes_accessed=seqs * seq_len * width * 14, transcendentals=square
        ),
    )(qkv, start, lses, grads)


def swap(values, axis):
    count = lax.axis_size(axis)
    return lax.ppermute(values, axis, [(i, i ^ 1) for i in range(count)])


def trade(values):
    return lax.all_to_all(values, CTX, split_axis=0, concat_axis=0, tiled=True)


def by_part(values, parts):
    return values.reshape(values.shape[0], parts, -1).transpose(1, 0, 2)


def by_row(values):
    return values.transpose(1, 0, 2).reshape(values.shape[1], -1)


def pair_sum(values):
    sent = values.astype(BF)
    return sent.astype(F32) + swap(sent, "tp").astype(F32)


def gather_rows(shard):
    part = lax.all_gather(shard, SAME, axis=0, tiled=False)
    other = swap(part, "core")
    core = lax.axis_index("core")
    low = jnp.where(core == 0, part, other)
    high = jnp.where(core == 0, other, part)
    return jnp.stack([low, high], axis=1).reshape(-1, shard.shape[1])


def core_sum(grad):
    groups = lax.axis_size("fsdp") * lax.axis_size("x")
    rows = grad.shape[0] // (2 * groups)
    core = lax.axis_index("core")
    halves = grad.astype(BF).reshape(groups, 2, rows, grad.shape[1])
    mine = lax.dynamic_index_in_dim(halves, core, 1, keepdims=False)
    theirs = lax.dynamic_index_in_dim(halves, 1 - core, 1, keepdims=False)
    summed = (mine.astype(F32) + swap(theirs, "core").astype(F32)).astype(BF)
    return summed.reshape(groups * rows, grad.shape[1])


def scatter_rows(summed):
    return lax.psum_scatter(summed, SAME, scatter_dimension=0, tiled=True).astype(F32)


def small_sums(*vectors):
    flat = jnp.concatenate([v.reshape(-1) for v in vectors])
    total = flat
    for axis in ALL:
        count = lax.axis_size(axis)
        step = 1
        while step < count:
            pairs = [(i, i ^ step) for i in range(count)]
            total = total + lax.ppermute(total, axis, pairs)
            step *= 2
    outs, at = [], 0
    for v in vectors:
        outs.append(total[at : at + v.size].reshape(v.shape))
        at += v.size
    return outs


def local(
    tokens,
    segment_ids,
    first_gain,
    first_shift,
    qkv_weight,
    qv_bias,
    out_weight,
    out_bias,
    second_gain,
    second_shift,
    up_weight,
    up_bias,
    down_weight,
    down_bias,
    cotangent,
):
    seqs, local_len, model = tokens.shape
    seq_len = segment_ids.shape[1]
    heads_cols = qkv_weight.shape[2]
    rows = seqs * local_len
    barrier = lax.optimization_barrier
    parts = lax.axis_size("x") * lax.axis_size("core")
    shard = qkv_weight.shape[1]
    width = heads_cols // parts
    qkv_rows = qkv_weight.reshape(3, shard, parts, width).transpose(1, 2, 0, 3)
    qkv_rows = qkv_rows.reshape(shard, 3 * heads_cols)
    first_set = gather_rows(jnp.concatenate([qkv_rows, out_weight.T], 1))
    w_qkv, w_out = first_set[:, : 3 * heads_cols], first_set[:, 3 * heads_cols :]
    units = up_weight.shape[1]
    second_set = gather_rows(jnp.concatenate([up_weight, down_weight.T], 1))
    w_up, w_down = second_set[:, :units], second_set[:, units:]

    start = jnp.sum(
        (segment_ids[:, None, :] < segment_ids[:, :, None]).astype(jnp.int32), -1
    )[:, None, :]
    inputs = tokens.astype(F32)
    normed_in, normed_one, inverse_one = norm_forward(inputs, first_gain, first_shift)
    first_in = normed_in.astype(BF)
    bias_row = jnp.stack([qv_bias[0], jnp.zeros_like(qv_bias[0]), qv_bias[1]])
    bias_row = bias_row.reshape(3, parts, width).transpose(1, 0, 2).reshape(-1)
    projected = (dot(first_in.reshape(rows, model), w_qkv, 1, 0) + bias_row).astype(BF)
    qkv = trade(by_part(projected, parts)).reshape(parts, seqs, local_len, 3 * width)
    attended, lses = attend_forward(qkv, start)
    mixed_rows = by_row(trade(attended.reshape(parts, rows, width)))

    attn_part = dot(mixed_rows, w_out, 1, 1).reshape(seqs, local_len, model)
    cot_rows = cotangent.reshape(rows, model)
    middle = inputs + pair_sum(attn_part) + out_bias
    normed_mid, normed_two, inverse_two = norm_forward(middle, second_gain, second_shift)
    second_in = normed_mid.astype(BF).reshape(rows, model)
    hidden_pre = dot(second_in, w_up, 1, 0) + up_bias
    activated, gate_pull = jax.vjp(smooth_gate, hidden_pre)
    hidden = activated.astype(BF)
    grad_hidden = dot(cot_rows, w_down, 1, 0)
    grad_pre = gate_pull(grad_hidden)[0]
    grad_pre_low = grad_pre.astype(BF)
    grad_up_b = jnp.sum(grad_pre, axis=0)
    grad_two_sum = pair_sum(dot(grad_pre_low, w_up, 1, 1).reshape(seqs, local_len, model))
    grad_top = cotangent.astype(F32)
    grad_mid_norm, grad_gain_two, grad_shift_two = norm_backward(
        grad_two_sum, normed_two, inverse_two, second_gain
    )
    grad_mid = grad_top + grad_mid_norm
    grad_mid_low = grad_mid.astype(BF).reshape(rows, model)
    grad_mixed = by_part(dot(grad_mid_low, w_out, 1, 0).astype(BF), parts)

    grad_down = dot(cot_rows, hidden, 0, 0).astype(BF)
    grad_up = dot(second_in, grad_pre_low, 0, 0).astype(BF)
    grad_out = dot(grad_mid_low, mixed_rows, 0, 0).astype(BF)
    down_part = dot(hidden, w_down, 1, 1).reshape(seqs, local_len, model)

    grad_att = trade(grad_mixed).reshape(parts, seqs, local_len, width)
    early = jnp.concatenate([grad_down, grad_up, grad_out], 1)
    grad_att, early, down_part = barrier((grad_att, core_sum(early), down_part.astype(BF)))
    own_early = scatter_rows(early)
    layer_out = (middle + pair_sum(down_part) + down_bias).astype(BF)
    grad_heads = attend_backward(qkv, start, lses, grad_att)
    grad_proj = by_row(trade(grad_heads.reshape(parts, rows, 3 * width)))
    grad_one_part = dot(grad_proj, w_qkv, 1, 1).reshape(seqs, local_len, model)
    grad_qkv = dot(first_in.reshape(rows, model), grad_proj, 0, 0)
    sent = grad_one_part.astype(BF)
    received, own_early, late = barrier((swap(sent, "tp"), own_early, core_sum(grad_qkv)))
    grad_one_sum = sent.astype(F32) + received.astype(F32)
    grad_in_norm, grad_gain_one, grad_shift_one = norm_backward(
        grad_one_sum, normed_one, inverse_one, first_gain
    )
    grad_inputs = grad_mid + grad_in_norm

    own_down = own_early[:, :units].T
    own_up = own_early[:, units : 2 * units]
    own_out = own_early[:, 2 * units :].T
    own_qkv = scatter_rows(late)
    own_qkv = own_qkv.reshape(shard, parts, 3, width).transpose(2, 0, 1, 3)
    own_qkv = own_qkv.reshape(3, shard, heads_cols)
    grad_qv_b = jnp.sum(grad_proj.astype(F32), axis=0).reshape(parts, 3, width)
    grad_qv_b = grad_qv_b.transpose(1, 0, 2).reshape(3, heads_cols)[0::2]
    sum_up_b, sum_down_b, sum_out_b, sum_gain_two, sum_shift_two = small_sums(
        grad_up_b,
        jnp.sum(grad_top, axis=(0, 1)),
        jnp.sum(grad_mid, axis=(0, 1)),
        grad_gain_two,
        grad_shift_two,
    )
    sum_qv_b, sum_gain_one, sum_shift_one = small_sums(grad_qv_b, grad_gain_one, grad_shift_one)
    return (
        layer_out,
        grad_inputs,
        sum_gain_one,
        sum_shift_one,
        own_qkv,
        sum_qv_b,
        own_out,
        sum_out_b,
        sum_gain_two,
        sum_shift_two,
        own_up,
        sum_up_b,
        own_down,
        sum_down_b,
    )


def solution(mesh):
    sizes = mesh.shape
    fine = Mesh(
        np.asarray(mesh.devices).reshape(sizes["fsdp"], sizes["ctx"] // 2, 2, sizes["tp"]),
        ("fsdp", "x", "core", "tp"),
    )
    return jax.shard_map(
        local,
        mesh=fine,
        in_specs=(
            P("fsdp", CTX, None),
            P("fsdp", None),
            P(),
            P(),
            P(None, ALL, "tp"),
            P(None, "tp"),
            P("tp", ALL),
            P(),
            P(),
            P(),
            P(ALL, "tp"),
            P("tp"),
            P("tp", ALL),
            P(),
            P("fsdp", CTX, None),
        ),
        out_specs=(
            P("fsdp", CTX, None),
            P("fsdp", CTX, None),
            P(),
            P(),
            P(None, ALL, "tp"),
            P(None, "tp"),
            P("tp", ALL),
            P(),
            P(),
            P(),
            P(ALL, "tp"),
            P("tp"),
            P("tp", ALL),
            P(),
        ),
        check_vma=False,
    )
```
